256 devices in a mesh: seq: 64 (over y, z, core), tp: 4 (over x).
Axes of the slice: x: 4, y: 4, z: 8, core: 2. Of those that a mesh axis runs over, the one named last changes fastest.
Arguments:
- queries: bfloat16 [98304, 2048], P('seq', 'tp'), may hold values from -160 to 160
- cotangent: bfloat16 [98304, 2048], P('seq', 'tp'), may hold values from -6 to 6
- owner_map: int32 [1536, 1], P('seq'), may hold values from 0 to 63; in each aligned block of 24 rows (0 to 23, 24 to 47, ...) at most 2 rows name the same one
- neighbour_ids: int32 [1536, 2], P('seq'), may hold values from 0 to 1
- database: bfloat16 [128, 128, 1536], P('seq', None, 'tp'), may hold values from -6 to 6
- norm_gain: float32 [1536], P('tp'), may hold values from 0.5 to 2
- key_weight: bfloat16 [1536, 2048], P(None, 'tp'), may hold values from -0.15625 to 0.15625
- value_weight: bfloat16 [1536, 2048], P(None, 'tp'), may hold values from -0.15625 to 0.15625
Outputs:
- attended: bfloat16 [98304, 2048], P('seq', 'tp')
- grad_key_weight: float32 [1536, 2048], P('seq', 'tp')
The draws below stay inside these ranges and needn't reach their ends.
Inputs may be any that keep to these rules, and one draw needn't show every extreme that they name: `owner_map`: in each aligned block of 24 spans (the spans of one index of seq) no owner is named more than 2 times, a bound that some block reaches.
All inputs are finite; a program needn't handle non-finite values.
Results may differ from the reference program's by a relative error of at most 0.01.
The reference program's roundings to bfloat16 on the way (of `normed`, `rounded_probs`, `grad_scores` and `rounded_grad_keys`) count: a program that leaves them out, or rounds other values in their place, can miss the bound.
Values may be sent and summed in bfloat16 or wider, within the bound.
No kernel may reach another device: no remote copies, remote signals or barrier semaphores. Data moves between devices by JAX's collectives and lax.ppermute only.
A program may use at most 128 MiB of HBM per device.

```python
import math
import jax
import jax.numpy as jnp
import numpy as np
from jax import lax

D_HEAD = 128
HEADS = 16
E = 1536
SPAN = 64
NB = 2
NLEN = 128
CH_DEV = 24
CAP = 2
DB_DEV = 2
TOKENS = 98304
SPANS = 1536
N_SEQ = 64


def draw_queries(key, part):
    key = jax.random.fold_in(key, 11)
    base_key = jax.random.fold_in(key, 0)
    normals = jax.random.normal(base_key, (TOKENS, HEADS * D_HEAD), jnp.float32)
    normals = jnp.clip(normals, -6.0, 6.0)
    return normals.astype(jnp.bfloat16)


def place_ends(drawn, key, smallest, top_value):
    longest = drawn.shape.index(max(drawn.shape))
    spots = []
    for shift in (0, 1):
        where = [jax.random.randint(jax.random.fold_in(key, axis), (), 0, length) for axis, length in enumerate(drawn.shape)]
        where[longest] = (where[longest] + shift) % drawn.shape[longest]
        spots.append(tuple(where))
    return drawn.at[spots[0]].set(smallest).at[spots[1]].set(top_value)


def steps_of(stream_key, dims, shards, smallest, largest):
    level = 1.0
    for dim, blocks in shards:
        heights = jax.random.uniform(jax.random.fold_in(jax.random.fold_in(stream_key, 6), dim), (blocks,), jnp.float32, smallest / len(shards), largest / len(shards))
        level = level * jnp.repeat(jnp.exp(heights), dims[dim] // blocks).reshape((-1,) + (1,) * (len(dims) - 1 - dim))
    return level


def deal_out(rng, own, number, rows, amount, top, most, lean):
    order = jax.random.permutation(rng, amount)
    crowded, usual = shares(amount, rows * top, most, lean, True), shares(amount, rows * top, most, lean, False)
    places = jnp.arange(amount)

    def named(lengths, turn):
        used = int((lengths > 0).sum())
        fixed = max(1, used // 4)
        moved = fixed + (places - fixed + turn * (used - fixed)) % max(1, amount - fixed)
        return jnp.zeros((amount,), jnp.int32).at[order[jnp.where(places < fixed, places, moved)]].set(jnp.asarray(lengths, jnp.int32))

    lengths = jnp.where(number % 4 == 0, named(crowded, number // 4), named(usual, number - number // 4 - 1))
    mixed = jax.random.permutation(jax.random.fold_in(own, 3), amount)
    donor, sink = mixed[0:amount // 2 * 2:2], mixed[1:amount // 2 * 2:2]
    margin = jnp.minimum(lengths[donor] - 1, most - lengths[sink]) // 2
    margin = jnp.where((donor == order[0]) | (sink == order[0]) | (lengths[sink] == 0), 0, jnp.maximum(margin, 0))
    moved = jax.random.randint(jax.random.fold_in(own, 4), (amount // 2,), 0, 1 << 20) % (margin + 1)
    lengths = lengths.at[donor].add(-moved).at[sink].add(moved)
    items = jnp.searchsorted(jnp.cumsum(lengths), jnp.arange(rows * top), side="right").astype(jnp.int32)
    grid = items.reshape(top, rows).T
    grid = grid[jax.random.permutation(jax.random.fold_in(own, 1), rows)]
    turn = jax.random.randint(jax.random.fold_in(own, 2), (rows, 1), 0, top)
    return jnp.take_along_axis(grid, (jnp.arange(top)[None, :] + turn) % top, axis=1)


def shares(number_of, total, limit, lean, full):
    loads = [(1 << 20) // math.isqrt(rank ** lean) + 1 for rank in range(1, number_of + 1)]
    largest = limit if full else min(limit, max(-(-total // number_of), total * loads[0] // sum(loads)))
    least = 1 if total - largest >= number_of - 1 else 0
    counts, surplus = [largest] + [least] * (number_of - 1), total - largest - least * (number_of - 1)
    while surplus > 0:
        movable = [i for i in range(1, number_of) if counts[i] < largest] or [i for i in range(1, number_of) if counts[i] < limit]
        whole, remaining = sum([loads[i] for i in movable]), surplus
        for i in movable:
            extra = min(limit - counts[i], max(1, remaining * loads[i] // whole), surplus)
            counts[i] = counts[i] + extra
            surplus = surplus - extra
    return np.array(counts)


def centred(stream_key, shape, deviation, bound, shards=(), kind=jnp.bfloat16):
    values = deviation * jax.random.normal(stream_key, shape, jnp.float32)
    if shards:
        values = values * steps_of(stream_key, shape, shards, -0.22, 0.18)
    return jnp.clip(values, -bound, bound).astype(kind)


def setup_inputs(seed: int = 0) -> dict:
    streams_of = jax.random.split(jax.random.key(seed), 9)
    queries = draw_queries(jax.random.fold_in(streams_of[8], 71), 0)
    cotangent = centred(streams_of[1], (TOKENS, HEADS * D_HEAD), 1.0, 6.0, ((0, 64), (1, 4)))
    owner_map_keys = jax.random.split(jax.random.fold_in(streams_of[2], 1), SPANS // CH_DEV)
    owner_map_turns = jax.random.permutation(jax.random.fold_in(streams_of[2], 3), SPANS // CH_DEV)
    owner_map = jax.vmap(lambda own, number: deal_out(jax.random.fold_in(streams_of[2], 2), own, number, CH_DEV, N_SEQ, 1, CAP, 2))(owner_map_keys, owner_map_turns).reshape((SPANS, 1))
    neighbour_ids = place_ends(jax.random.randint(streams_of[3], (SPANS, NB), 0, DB_DEV), jax.random.fold_in(streams_of[3], 1), 0, DB_DEV - 1).astype(jnp.int32)
    database = centred(streams_of[4], (DB_DEV * N_SEQ, NLEN, E), 1.0, 6.0, ((0, 64), (2, 4)))
    norm_gain = jnp.clip(jnp.exp(math.log(2.0) - 1.3862944 * jax.random.uniform(streams_of[5], (E,), jnp.float32) ** steps_of(streams_of[5], (E,), ((0, 4),), -0.2, 0.2)), 0.5, 2.0)
    key_weight = centred(streams_of[6], (E, HEADS * D_HEAD), E ** -0.5, 0.15625, ((1, 4),))
    value_weight = centred(streams_of[7], (E, HEADS * D_HEAD), E ** -0.5, 0.15625, ((1, 4),))
    return dict(queries=queries, cotangent=cotangent, owner_map=owner_map, neighbour_ids=neighbour_ids, database=database, norm_gain=norm_gain, key_weight=key_weight, value_weight=value_weight)


epsilon = 1e-06

def reference(queries, cotangent, owner_map, neighbour_ids, database, norm_gain, key_weight, value_weight):
    floats = database.astype(jnp.float32)
    factor = lax.rsqrt(lax.optimization_barrier(jnp.mean(floats * floats, axis=2, keepdims=True)) + epsilon)
    normed = (floats * factor * norm_gain.astype(jnp.float32)).astype(jnp.bfloat16)
    normed_rows = normed.reshape(DB_DEV * N_SEQ * NLEN, E)
    key_rows = jnp.dot(normed_rows, key_weight, preferred_element_type=jnp.float32).astype(jnp.bfloat16)
    value_rows = jnp.dot(normed_rows, value_weight, preferred_element_type=jnp.float32).astype(jnp.bfloat16)
    key_rows = key_rows.reshape(DB_DEV * N_SEQ, NLEN, HEADS, D_HEAD)
    value_rows = value_rows.reshape(DB_DEV * N_SEQ, NLEN, HEADS, D_HEAD)
    listed = (owner_map[:, 0:1] * DB_DEV + neighbour_ids).astype(jnp.int32)
    block_size = math.gcd(SPANS, 16)
    block_count = SPANS // block_size
    query_all = queries.reshape(block_count, block_size, SPAN, HEADS, D_HEAD)
    cot_all = cotangent.reshape(block_count, block_size, SPAN, HEADS, D_HEAD)
    listed_all = listed.reshape(block_count, block_size, NB)
    inv_root = 1.0 / math.sqrt(D_HEAD)

    def advance(running, inputs):
        query_block, cot_block, listed_block = inputs
        seen_keys = key_rows[listed_block].reshape(block_size, NB * NLEN, HEADS, D_HEAD).astype(jnp.float32)
        seen_values = value_rows[listed_block].reshape(block_size, NB * NLEN, HEADS, D_HEAD).astype(jnp.float32)
        query_wide = query_block.astype(jnp.float32)
        scores = jnp.einsum('cqhd,ckhd->chqk', query_wide, seen_keys) * inv_root
        probabilities = jax.nn.softmax(scores, axis=3)
        rounded_probs = lax.optimization_barrier(probabilities.astype(jnp.bfloat16)).astype(jnp.float32)
        attended_block = jnp.einsum('chqk,ckhd->cqhd', rounded_probs, seen_values).astype(jnp.bfloat16)
        grad_probs = jnp.einsum('cqhd,ckhd->chqk', cot_block.astype(jnp.float32), seen_values)
        row_delta = lax.optimization_barrier(jnp.sum(probabilities * grad_probs, axis=3, keepdims=True))
        grad_scores = (probabilities * (grad_probs - row_delta) * inv_root).astype(jnp.bfloat16)
        grad_scores = lax.optimization_barrier(grad_scores).astype(jnp.float32)
        grad_keys = jnp.einsum('chqk,cqhd->ckhd', grad_scores, query_wide)
        grad_keys = grad_keys.reshape(block_size * NB, NLEN, HEADS, D_HEAD)
        running = running.at[listed_block.reshape(-1).astype(jnp.int32)].add(grad_keys)
        return (running, attended_block)
    start = jnp.zeros((DB_DEV * N_SEQ, NLEN, HEADS, D_HEAD), jnp.float32)
    totals, attended = lax.scan(advance, start, (query_all, cot_all, listed_all))
    attended = attended.reshape(TOKENS, HEADS * D_HEAD)
    rounded_grad_keys = totals.astype(jnp.bfloat16).reshape(DB_DEV * N_SEQ * NLEN, HEADS * D_HEAD)
    grad_key_weight = jnp.dot(normed_rows.T, rounded_grad_keys, preferred_element_type=jnp.float32)
    return (attended, grad_key_weight)
```

```python
import functools
import math

import jax
import jax.numpy as jnp
from jax import lax
from jax.experimental import pallas as pl
from jax.experimental.pallas import tpu as pltpu
from jax.sharding import PartitionSpec as P

D_HEAD = 128
SPAN = 64
NLEN = 128
N_Y, N_Z = 4, 8
CHIPS = N_Y * N_Z
SLOTS = 4
CHUNKS = 2
epsilon = 1e-06


def seq_of(y, z, core):
    return ((y % N_Y) * N_Z + z % N_Z) * 2 + core


PAIR = [(i, i ^ 1) for i in range(2 * CHIPS)]
SAME_CORE = [[seq_of(y, z, c) for y in range(N_Y) for z in range(N_Z)] for c in range(2)]
Z_GROUPS = [[seq_of(y, z, c) for z in range(N_Z)] for y in range(N_Y) for c in range(2)]
Y_GROUPS = [[seq_of(y, z, c) for y in range(N_Y)] for z in range(N_Z) for c in range(2)]


def swap(x):
    return lax.ppermute(x, "seq", PAIR)


def gather_chips(x):
    return lax.all_gather(x, "seq", axis_index_groups=SAME_CORE, axis=0, tiled=False)


def scatter_chips(x):
    rest = x.shape[1:]
    x = x.reshape(N_Y, N_Z * rest[0], *rest[1:])
    x = lax.psum_scatter(x, "seq", axis_index_groups=Y_GROUPS, scatter_dimension=0, tiled=False)
    x = x.reshape(N_Z, *rest)
    return lax.psum_scatter(x, "seq", axis_index_groups=Z_GROUPS, scatter_dimension=0, tiled=False)


def tables(owners, core):
    spans = owners.shape[0]
    order = jnp.arange(spans)
    same = owners[:, None] == owners[None, :]
    position = jnp.sum((same & (order[None, :] < order[:, None])).astype(jnp.int32), axis=1)
    wanted = 2 * jnp.arange(CHIPS) + core
    match = (wanted[:, None] == owners[None, :])[:, None, :] & (
        position[None, None, :] == jnp.arange(SLOTS)[None, :, None]
    )
    slot = jnp.sum(jnp.where(match, order[None, None, :], 0), axis=2)
    count = jnp.sum(match.astype(jnp.int32), axis=(1, 2))
    return count.astype(jnp.int32), slot.reshape(-1).astype(jnp.int32)


def attention_kernel(heads, count, slot, ids, q_ref, cot_ref, kv_ref, att_ref, grad_ref, acc):
    owner = pl.program_id(0)
    inv_root = 1.0 / math.sqrt(D_HEAD)
    acc[...] = jnp.zeros_like(acc)
    first_half = lax.broadcasted_iota(jnp.int32, (1, 2 * NLEN), 1) < NLEN

    def one_span(k, carry):
        span = slot[owner * SLOTS + k]
        rows = pl.ds(pl.multiple_of(span * SPAN, SPAN), SPAN)
        one, two = ids[2 * span], ids[2 * span + 1]
        low = jnp.where((one == 0) | (two == 0), 0.0, -1e30)
        high = jnp.where((one == 1) | (two == 1), 0.0, -1e30)
        bias = jnp.where(first_half, low, high)
        for h in range(heads):
            cols = slice(h * D_HEAD, (h + 1) * D_HEAD)
            q = q_ref[rows, cols]
            cot = cot_ref[rows, cols]
            key = kv_ref[0, :, cols]
            value = kv_ref[0, :, (heads + h) * D_HEAD : (heads + h + 1) * D_HEAD]
            scores = lax.dot_general(
                q, key, (((1,), (1,)), ((), ())), preferred_element_type=jnp.float32
            )
            scores = scores * (inv_root * math.log2(math.e)) + bias
            weights = jnp.exp2(scores - jnp.max(scores, axis=1, keepdims=True))
            probs = weights * (1.0 / jnp.sum(weights, axis=1, keepdims=True))
            att = jnp.dot(probs.astype(jnp.bfloat16), value, preferred_element_type=jnp.float32)
            att_ref[rows, cols] = att.astype(jnp.bfloat16)
            grad_probs = lax.dot_general(
                cot, value, (((1,), (1,)), ((), ())), preferred_element_type=jnp.float32
            )
            delta = jnp.sum(probs * grad_probs, axis=1, keepdims=True)
            grad_scores = (probs * (grad_probs - delta) * inv_root).astype(jnp.bfloat16)
            acc[h] += lax.dot_general(
                q, grad_scores, (((0,), (0,)), ((), ())), preferred_element_type=jnp.float32
            )
        return carry

    lax.fori_loop(0, count[owner], one_span, 0)
    grad_ref[0] = acc[...].reshape(heads * D_HEAD, 2 * NLEN).astype(jnp.bfloat16)


def attend(count, slot, ids, q, cot, kv, chunk):
    heads = kv.shape[2] // (2 * D_HEAD)
    width = heads * D_HEAD
    rows = q.shape[0]
    seen = kv.shape[1]
    return pl.pallas_call(
        functools.partial(attention_kernel, heads),
        grid_spec=pltpu.PrefetchScalarGridSpec(
            num_scalar_prefetch=3,
            grid=(CHIPS,),
            in_specs=[
                pl.BlockSpec((rows, width), lambda o, *_: (0, chunk)),
                pl.BlockSpec((rows, width), lambda o, *_: (0, chunk)),
                pl.BlockSpec((1, seen, 2 * width), lambda o, *_: (o, 0, 0)),
            ],
            out_specs=[
                pl.BlockSpec((rows, width), lambda o, *_: (0, 0)),
                pl.BlockSpec((1, width, seen), lambda o, *_: (o, 0, 0)),
            ],
            scratch_shapes=[pltpu.VMEM((heads, D_HEAD, seen), jnp.float32)],
        ),
        out_shape=[
            jax.ShapeDtypeStruct((rows, width), jnp.bfloat16),
            jax.ShapeDtypeStruct((CHIPS, width, seen), jnp.bfloat16),
        ],
        compiler_params=pltpu.CompilerParams(vmem_limit_bytes=40 * 1024 * 1024),
        cost_estimate=pl.CostEstimate(
            flops=rows * seen * width * 4, bytes_accessed=12 * 1024 * 1024, transcendentals=rows * seen * heads
        ),
    )(count, slot, ids, q, cot, kv)


def normed_store(database, norm_gain):
    rows = database.reshape(-1, database.shape[2])
    stored = rows.shape[0]
    top = lax.reduce_precision(norm_gain, 8, 7)
    middle = lax.reduce_precision(norm_gain - top, 8, 7)
    bottom = norm_gain - top - middle
    gains = jnp.stack([top, middle, bottom]).astype(jnp.bfloat16)
    packed = jnp.concatenate([rows, jnp.pad(gains, ((0, 13), (0, 0)))], axis=0)
    whole = lax.all_gather(packed, "tp", axis=1, tiled=True).astype(jnp.float32)
    floats = whole[:stored]
    gain = whole[stored] + whole[stored + 1] + whole[stored + 2]
    mean = jnp.sum(floats * floats, axis=1, keepdims=True) / floats.shape[1]
    return (floats * lax.rsqrt(mean + epsilon) * gain[None, :]).astype(jnp.bfloat16)


def scatter_gradient(grad):
    width = grad.shape[1]
    core = lax.axis_index("seq") % 2
    parts = grad.reshape(CHIPS, 2, -1, width)
    mine = lax.dynamic_index_in_dim(parts, core, 1, keepdims=False)
    other = lax.dynamic_index_in_dim(parts, 1 - core, 1, keepdims=False)
    total = mine + swap(other.astype(jnp.bfloat16)).astype(jnp.float32)
    for groups in (Y_GROUPS, Z_GROUPS):
        size = len(groups[0])
        total = total.astype(jnp.bfloat16).reshape(size, -1, parts.shape[2], width)
        total = lax.all_to_all(total, "seq", 0, 0, axis_index_groups=groups, tiled=True)
        total = jnp.sum(total.astype(jnp.float32), axis=0)
    return total.reshape(parts.shape[2], width)


def per_device(
    queries, cotangent, owner_map, neighbour_ids, database, norm_gain, key_weight, value_weight
):
    core = lax.axis_index("seq") % 2
    tokens, local_width = queries.shape
    width = local_width // CHUNKS

    meta = jnp.concatenate([owner_map, neighbour_ids], axis=1)
    meta = jnp.concatenate([meta, swap(meta)], axis=0)
    q = jnp.concatenate([queries, swap(queries)], axis=0)
    cot = jnp.concatenate([cotangent, swap(cotangent)], axis=0)
    owners, ids = meta[:, 0], meta[:, 1:].reshape(-1)
    count, slot = tables(owners, core)

    normed = normed_store(database, norm_gain)
    key_rows = jnp.dot(normed, key_weight, preferred_element_type=jnp.float32).astype(jnp.bfloat16)
    value_rows = jnp.dot(normed, value_weight, preferred_element_type=jnp.float32).astype(
        jnp.bfloat16
    )

    here = (owner_map % 2) == core
    here = jnp.broadcast_to(here, (here.shape[0], SPAN)).reshape(tokens, 1)
    attended, grads = [], []
    for chunk in range(CHUNKS):
        cols = slice(chunk * width, (chunk + 1) * width)
        kv = jnp.concatenate([key_rows[:, cols], value_rows[:, cols]], axis=1)
        kv = gather_chips(kv)
        att, grad_keys = attend(count, slot, ids, q, cot, kv, chunk)
        attended.append(jnp.where(here, att[:tokens], swap(att[tokens:])))
        grad_keys = scatter_chips(grad_keys)
        grad = lax.dot_general(
            normed, grad_keys, (((0,), (1,)), ((), ())), preferred_element_type=jnp.float32
        )
        grads.append(scatter_gradient(grad))
    return jnp.concatenate(attended, axis=1), jnp.concatenate(grads, axis=1)


def solution(mesh):
    placed = (
        P("seq", "tp"),
        P("seq", "tp"),
        P("seq", None),
        P("seq", None),
        P("seq", None, "tp"),
        P("tp"),
        P(None, "tp"),
        P(None, "tp"),
    )
    return jax.shard_map(
        per_device,
        mesh=mesh,
        in_specs=placed,
        out_specs=(P("seq", "tp"), P("seq", "tp")),
        check_vma=False,
    )
```

```python
import functools
import math

import jax
import jax.numpy as jnp
from jax import lax
from jax.experimental import pallas as pl
from jax.experimental.pallas import tpu as pltpu
from jax.sharding import PartitionSpec as P

D_HEAD = 128
SPAN = 64
NLEN = 128
N_Y, N_Z = 4, 8
CHIPS = N_Y * N_Z
TOGETHER = 4
epsilon = 1e-06


def seq_of(y, z, core):
    return ((y % N_Y) * N_Z + z % N_Z) * 2 + core


PAIR = [(i, i ^ 1) for i in range(2 * CHIPS)]
Z_GROUPS = [[seq_of(y, z, c) for z in range(N_Z)] for y in range(N_Y) for c in range(2)]
Y_GROUPS = [[seq_of(y, z, c) for y in range(N_Y)] for z in range(N_Z) for c in range(2)]
CELLS = [(y, z, c) for y in range(N_Y) for z in range(N_Z) for c in range(2)]
NT = (((1,), (1,)), ((), ()))
TN = (((0,), (0,)), ((), ()))


def swap(x):
    return lax.ppermute(x, "seq", PAIR)


def from_y(x, step):
    return lax.ppermute(x, "seq", [(seq_of(y + step, z, c), seq_of(y, z, c)) for y, z, c in CELLS])


def from_z(x, step):
    return lax.ppermute(x, "seq", [(seq_of(y, z + step, c), seq_of(y, z, c)) for y, z, c in CELLS])


def add(x, *others):
    total = x.astype(jnp.float32)
    for other in others:
        total = total + other.astype(jnp.float32)
    return total.astype(jnp.bfloat16)


def halves(x):
    middle = x.shape[0] // 2
    return x[:middle], x[middle:]


def ring_gather(x, fetch, size):
    up, down, parts = x, x, [x]
    for unused in range(size // 2 - 1):
        up, down = fetch(up, 1), fetch(down, -1)
        parts += [up, down]
    return parts + [fetch(halves(up)[0], 1), fetch(halves(down)[1], -1)]


def ring_scatter(parts, fetch, size):
    first, second = fetch(parts[-2], -1), fetch(parts[-1], 1)
    plus, minus = parts[size - 3], parts[size - 2]
    plus = jnp.concatenate([add(halves(plus)[0], first), halves(plus)[1]])
    minus = jnp.concatenate([halves(minus)[0], add(halves(minus)[1], second)])
    for hop in range(size // 2 - 2, 0, -1):
        plus, minus = (
            add(parts[2 * hop - 1], fetch(plus, -1)),
            add(parts[2 * hop], fetch(minus, 1)),
        )
    return add(parts[0], fetch(plus, -1), fetch(minus, 1))


def ring_place(offset, size):
    offset = offset % size
    place = jnp.where(offset < size // 2, 2 * offset - 1, 2 * (size - offset))
    place = jnp.where(offset == size // 2, size - 1, place)
    return jnp.where(offset == 0, 0, place)


def work_list(place, member, first, last):
    spans = place.shape[0]
    chosen = member & (place >= first) & (place < last)
    order = jnp.arange(spans)
    before = order[None, :] < order[:, None]
    rank = jnp.sum((before & chosen[None, :]).astype(jnp.int32), axis=1)
    at = chosen[None, :] & (rank[None, :] == order[:, None])
    listed = jnp.sum(jnp.where(at, order[None, :], 0), axis=1)
    block = jnp.sum(jnp.where(at, place[None, :] - first, 0), axis=1)
    number = jnp.sum(chosen.astype(jnp.int32)).reshape(1)
    return number, listed.astype(jnp.int32), block.astype(jnp.int32)


def attention_kernel(heads, sizes, earlier, number, listed, block, ids, *refs):
    parts = len(sizes)
    q_ref, cot_ref = refs[:2]
    sources = refs[2 : 2 + parts]
    refs = refs[2 + parts :]
    if earlier:
        before_ref, refs = refs[0], refs[1:]
    att_ref, refs = refs[0], refs[1:]
    grad_refs = refs[:parts]
    kv, acc, semaphores = refs[parts:]
    inv_root = 1.0 / math.sqrt(D_HEAD)
    dot = functools.partial(lax.dot_general, preferred_element_type=jnp.float32)

    copies, start = [], 0
    for i, size in enumerate(sizes):
        copies.append(
            pltpu.make_async_copy(sources[i], kv.at[pl.ds(start, size)], semaphores.at[i])
        )
        copies[-1].start()
        start += size
    acc[...] = jnp.zeros_like(acc)
    if earlier:
        att_ref[...] = before_ref[...]
    for copy in copies:
        copy.wait()

    first_half = lax.broadcasted_iota(jnp.int32, (1, 2 * NLEN), 1) < NLEN
    amount = number[0]
    key_cols = [slice(h * D_HEAD, (h + 1) * D_HEAD) for h in range(heads)]
    value_cols = [slice((heads + h) * D_HEAD, (heads + h + 1) * D_HEAD) for h in range(heads)]

    def step(i, carry):
        items = []
        for u in range(TOGETHER):
            k = i * TOGETHER + u
            at = jnp.minimum(k, amount - 1)
            span, place = listed[at], block[at]
            rows = pl.ds(pl.multiple_of(span * SPAN, SPAN), SPAN)
            one, two = ids[2 * span], ids[2 * span + 1]
            low = jnp.where((one == 0) | (two == 0), 0.0, -1e30)
            high = jnp.where((one == 1) | (two == 1), 0.0, -1e30)
            bias = jnp.where(first_half, low, high)
            scale = jnp.where(k < amount, inv_root, 0.0)
            items += [(rows, place, bias, scale, h) for h in range(heads)]
        q = [q_ref[rows, key_cols[h]] for rows, _, _, _, h in items]
        scores = [
            dot(x, kv[place, :, key_cols[h]], NT) * (inv_root * math.log2(math.e)) + bias
            for x, (_, place, bias, _, h) in zip(q, items)
        ]
        grad_probs = [
            dot(cot_ref[rows, key_cols[h]], kv[place, :, value_cols[h]], NT)
            for rows, place, _, _, h in items
        ]
        highest = [jnp.max(s, axis=1, keepdims=True) for s in scores]
        weights = [jnp.exp2(s - m) for s, m in zip(scores, highest)]
        sums = [jnp.sum(w, axis=1, keepdims=True) for w in weights]
        probs = [w * (1.0 / s) for w, s in zip(weights, sums)]
        deltas = [jnp.sum(p * g, axis=1, keepdims=True) for p, g in zip(probs, grad_probs)]
        grad_scores = [
            (p * (g - d) * item[3]).astype(jnp.bfloat16)
            for p, g, d, item in zip(probs, grad_probs, deltas, items)
        ]
        for p, (rows, place, _, _, h) in zip(probs, items):
            att = jnp.dot(
                p.astype(jnp.bfloat16),
                kv[place, :, value_cols[h]],
                preferred_element_type=jnp.float32,
            )
            att_ref[rows, key_cols[h]] = att.astype(jnp.bfloat16)
        for x, g, (_, place, _, _, h) in zip(q, grad_scores, items):
            acc[place, key_cols[h]] += dot(x, g, TN)
        return carry

    lax.fori_loop(0, (amount + TOGETHER - 1) // TOGETHER, step, 0)

    start = 0
    for ref, size in zip(grad_refs, sizes):

        def round_block(b, carry, ref=ref, start=start):
            ref[b] = acc[start + b].astype(jnp.bfloat16)
            return carry

        lax.fori_loop(0, size, round_block, 0)
        start += size


def attend(work, ids, q, cot, column, parts, earlier=None):
    seen, width = parts[0].shape[1], parts[0].shape[2] // 2
    heads, tokens = width // D_HEAD, q.shape[0]
    sizes = [part.shape[0] for part in parts]
    whole = pl.BlockSpec((tokens, width), lambda i, *_: (0, 0))
    chunk = pl.BlockSpec((tokens, width), lambda i, *_: (0, column))
    before = [] if earlier is None else [earlier]
    out = pl.pallas_call(
        functools.partial(attention_kernel, heads, sizes, bool(before)),
        grid_spec=pltpu.PrefetchScalarGridSpec(
            num_scalar_prefetch=4,
            grid=(1,),
            in_specs=[chunk, chunk]
            + [pl.BlockSpec(memory_space=pl.ANY)] * len(parts)
            + [whole] * len(before),
            out_specs=[whole]
            + [pl.BlockSpec((size, width, seen), lambda i, *_: (0, 0, 0)) for size in sizes],
            scratch_shapes=[
                pltpu.VMEM((sum(sizes), seen, 2 * width), jnp.bfloat16),
                pltpu.VMEM((sum(sizes), width, seen), jnp.float32),
                pltpu.SemaphoreType.DMA((len(sizes),)),
            ],
        ),
        out_shape=[jax.ShapeDtypeStruct((tokens, width), jnp.bfloat16)]
        + [jax.ShapeDtypeStruct((size, width, seen), jnp.bfloat16) for size in sizes],
        compiler_params=pltpu.CompilerParams(vmem_limit_bytes=48 * 1024 * 1024),
        cost_estimate=pl.CostEstimate(
            flops=tokens * seen * width * 4,
            bytes_accessed=sum(sizes) * seen * width * 6 + tokens * width * 6,
            transcendentals=tokens * seen * heads,
        ),
    )(*work, ids, q, cot, *parts, *before)
    return out[0], out[1:]


def normed_store(database, norm_gain):
    rows = database.reshape(-1, database.shape[2])
    stored = rows.shape[0]
    top = lax.reduce_precision(norm_gain, 8, 7)
    middle = lax.reduce_precision(norm_gain - top, 8, 7)
    bottom = norm_gain - top - middle
    gains = jnp.stack([top, middle, bottom]).astype(jnp.bfloat16)
    packed = jnp.concatenate([rows, jnp.pad(gains, ((0, 13), (0, 0)))], axis=0)
    whole = lax.all_gather(packed, "tp", axis=1, tiled=True).astype(jnp.float32)
    floats = whole[:stored]
    gain = whole[stored] + whole[stored + 1] + whole[stored + 2]
    mean = jnp.sum(floats * floats, axis=1, keepdims=True) / floats.shape[1]
    return (floats * lax.rsqrt(mean + epsilon) * gain[None, :]).astype(jnp.bfloat16)


def scatter_gradient(grad):
    width = grad.shape[1]
    core = lax.axis_index("seq") % 2
    parts = grad.reshape(CHIPS, 2, -1, width)
    mine = lax.dynamic_index_in_dim(parts, core, 1, keepdims=False)
    other = lax.dynamic_index_in_dim(parts, 1 - core, 1, keepdims=False)
    total = mine + swap(other.astype(jnp.bfloat16)).astype(jnp.float32)
    for groups in (Y_GROUPS, Z_GROUPS):
        size = len(groups[0])
        total = total.astype(jnp.bfloat16).reshape(size, -1, parts.shape[2], width)
        total = lax.all_to_all(total, "seq", 0, 0, axis_index_groups=groups, tiled=True)
        total = jnp.sum(total.astype(jnp.float32), axis=0)
    return total.reshape(parts.shape[2], width)


def per_device(
    queries, cotangent, owner_map, neighbour_ids, database, norm_gain, key_weight, value_weight
):
    core = lax.axis_index("seq") % 2
    tokens, local_width = queries.shape
    width = local_width // 2

    meta = jnp.concatenate([owner_map, neighbour_ids], axis=1)
    meta = jnp.concatenate([meta, swap(meta)], axis=0)
    q = jnp.concatenate([queries, swap(queries)], axis=0)
    cot = jnp.concatenate([cotangent, swap(cotangent)], axis=0)
    owners, ids = meta[:, 0], meta[:, 1:].reshape(-1)
    chip = lax.axis_index("seq") // 2
    member = owners % 2 == core
    y_place = ring_place(owners // (2 * N_Z) - chip // N_Z, N_Y)
    z_place = ring_place(owners // 2 - chip, N_Z)

    normed = normed_store(database, norm_gain)
    key_rows = jnp.dot(normed, key_weight, preferred_element_type=jnp.float32).astype(jnp.bfloat16)
    value_rows = jnp.dot(normed, value_weight, preferred_element_type=jnp.float32).astype(
        jnp.bfloat16
    )

    kv = [
        jnp.concatenate([r[:, i * width : (i + 1) * width] for r in (key_rows, value_rows)], axis=1)
        for i in range(2)
    ]

    line = ring_gather(kv[0], from_z, N_Z)
    line = jnp.stack(line[:-2] + [jnp.concatenate(line[-2:])])
    parts = ring_gather(line, from_y, N_Y)
    place = y_place * N_Z + z_place
    work = functools.partial(work_list, place, member)
    near, grads_near = attend(work(0, 3 * N_Z), ids, q, cot, 0, parts[:3])
    att_one, grads_far = attend(work(3 * N_Z, CHIPS), ids, q, cot, 0, parts[3:], near)
    sums = ring_scatter(list(grads_near) + list(grads_far), from_y, N_Y)
    grad_one = ring_scatter([*sums[:-1], *halves(sums[-1])], from_z, N_Z)

    line = ring_gather(kv[1], from_y, N_Y)
    line = jnp.stack(line[:-2] + [jnp.concatenate(line[-2:])])
    parts = ring_gather(line, from_z, N_Z)
    place = z_place * N_Y + y_place
    work = functools.partial(work_list, place, member)
    near, grads_near = attend(work(0, 5 * N_Y), ids, q, cot, 1, parts[:5])
    att_two, grads_far = attend(work(5 * N_Y, CHIPS), ids, q, cot, 1, parts[5:], near)
    sums = ring_scatter(list(grads_near) + list(grads_far), from_z, N_Z)
    grad_two = ring_scatter([*sums[:-1], *halves(sums[-1])], from_y, N_Y)

    here = owner_map % 2 == core
    here = jnp.broadcast_to(here, (here.shape[0], SPAN)).reshape(tokens, 1)
    attended = [jnp.where(here, att[:tokens], swap(att[tokens:])) for att in (att_one, att_two)]
    grad_keys = jnp.concatenate([grad_one, grad_two], axis=0)
    grad = lax.dot_general(
        normed, grad_keys, (((0,), (1,)), ((), ())), preferred_element_type=jnp.float32
    )
    return jnp.concatenate(attended, axis=1), scatter_gradient(grad)


def solution(mesh):
    placed = (
        P("seq", "tp"),
        P("seq", "tp"),
        P("seq", None),
        P("seq", None),
        P("seq", None, "tp"),
        P("tp"),
        P(None, "tp"),
        P(None, "tp"),
    )
    return jax.shard_map(
        per_device,
        mesh=mesh,
        in_specs=placed,
        out_specs=(P("seq", "tp"), P("seq", "tp")),
        check_vma=False,
    )
```

```python
import functools
import math

import jax
import jax.numpy as jnp
from jax import lax
from jax.experimental import pallas as pl
from jax.experimental.pallas import tpu as pltpu
from jax.sharding import PartitionSpec as P

D_HEAD = 128
SPAN = 64
NLEN = 128
N_Y, N_Z = 4, 8
CHIPS = N_Y * N_Z
TOGETHER = 4
epsilon = 1e-06


def seq_of(y, z, core):
    return ((y % N_Y) * N_Z + z % N_Z) * 2 + core


PAIR = [(i, i ^ 1) for i in range(2 * CHIPS)]
Z_GROUPS = [[seq_of(y, z, c) for z in range(N_Z)] for y in range(N_Y) for c in range(2)]
Y_GROUPS = [[seq_of(y, z, c) for y in range(N_Y)] for z in range(N_Z) for c in range(2)]
CELLS = [(y, z, c) for y in range(N_Y) for z in range(N_Z) for c in range(2)]
NT = (((1,), (1,)), ((), ()))
TN = (((0,), (0,)), ((), ()))


def swap(x):
    with jax.named_scope("swap"):
        return lax.ppermute(x, "seq", PAIR)


def from_y(x, step):
    with jax.named_scope("y"):
        return lax.ppermute(x, "seq", [(seq_of(y + step, z, c), seq_of(y, z, c)) for y, z, c in CELLS])


def from_z(x, step):
    with jax.named_scope("z"):
        return lax.ppermute(x, "seq", [(seq_of(y, z + step, c), seq_of(y, z, c)) for y, z, c in CELLS])


def add(x, *others):
    total = x.astype(jnp.float32)
    for other in others:
        total = total + other.astype(jnp.float32)
    return total.astype(jnp.bfloat16)


def after(values, done):
    return lax.optimization_barrier((values, done))[0]


def halves(x):
    middle = x.shape[0] // 2
    return x[:middle], x[middle:]


def ring_near(x, fetch, size):
    up, down, parts = x, x, [x]
    for hop in range(1, size // 2):
        with jax.named_scope(f"gather_{hop}"):
            up, down = fetch(up, 1), fetch(down, -1)
        parts += [up, down]
    return parts


def ring_far(parts, fetch):
    with jax.named_scope("gather_far"):
        return [fetch(halves(parts[-2])[0], 1), fetch(halves(parts[-1])[1], -1)]


def ring_gather(x, fetch, size):
    parts = ring_near(x, fetch, size)
    return parts + ring_far(parts, fetch)


def join(parts):
    return jnp.stack(parts[:-2] + [jnp.concatenate(parts[-2:])])


def ring_scatter(parts, fetch, size):
    with jax.named_scope("scatter_far"):
        first, second = fetch(parts[-2], -1), fetch(parts[-1], 1)
    plus, minus = parts[size - 3], parts[size - 2]
    plus = jnp.concatenate([add(halves(plus)[0], first), halves(plus)[1]])
    minus = jnp.concatenate([halves(minus)[0], add(halves(minus)[1], second)])
    for hop in range(size // 2 - 2, 0, -1):
        with jax.named_scope(f"scatter_{hop + 1}"):
            plus, minus = (
                add(parts[2 * hop - 1], fetch(plus, -1)),
                add(parts[2 * hop], fetch(minus, 1)),
            )
    with jax.named_scope("scatter_1"):
        return add(parts[0], fetch(plus, -1), fetch(minus, 1))


def ring_place(offset, size):
    offset = offset % size
    place = jnp.where(offset < size // 2, 2 * offset - 1, 2 * (size - offset))
    place = jnp.where(offset == size // 2, size - 1, place)
    return jnp.where(offset == 0, 0, place)


def work_list(place, member, first, last):
    spans = place.shape[0]
    chosen = member & (place >= first) & (place < last)
    order = jnp.arange(spans)
    before = order[None, :] < order[:, None]
    rank = jnp.sum((before & chosen[None, :]).astype(jnp.int32), axis=1)
    at = chosen[None, :] & (rank[None, :] == order[:, None])
    listed = jnp.sum(jnp.where(at, order[None, :], 0), axis=1)
    block = jnp.sum(jnp.where(at, place[None, :] - first, 0), axis=1)
    number = jnp.sum(chosen.astype(jnp.int32)).reshape(1)
    return number, listed.astype(jnp.int32), block.astype(jnp.int32)


def attention_kernel(heads, sizes, earlier, number, listed, block, ids, *refs):
    parts = len(sizes)
    q_ref, cot_ref = refs[:2]
    sources = refs[2 : 2 + parts]
    refs = refs[2 + parts :]
    if earlier:
        before_ref, refs = refs[0], refs[1:]
    att_ref, refs = refs[0], refs[1:]
    grad_refs = refs[:parts]
    kv, acc, semaphores = refs[parts:]
    inv_root = 1.0 / math.sqrt(D_HEAD)
    dot = functools.partial(lax.dot_general, preferred_element_type=jnp.float32)

    copies, start = [], 0
    for i, size in enumerate(sizes):
        copies.append(
            pltpu.make_async_copy(sources[i], kv.at[pl.ds(start, size)], semaphores.at[i])
        )
        copies[-1].start()
        start += size
    acc[...] = jnp.zeros_like(acc)
    if earlier:
        att_ref[...] = before_ref[...]
    for copy in copies:
        copy.wait()

    first_half = lax.broadcasted_iota(jnp.int32, (1, 2 * NLEN), 1) < NLEN
    amount = number[0]
    key_cols = [slice(h * D_HEAD, (h + 1) * D_HEAD) for h in range(heads)]
    value_cols = [slice((heads + h) * D_HEAD, (heads + h + 1) * D_HEAD) for h in range(heads)]

    def step(i, carry):
        items = []
        for u in range(TOGETHER):
            k = i * TOGETHER + u
            at = jnp.minimum(k, amount - 1)
            span, place = listed[at], block[at]
            rows = pl.ds(pl.multiple_of(span * SPAN, SPAN), SPAN)
            one, two = ids[2 * span], ids[2 * span + 1]
            low = jnp.where((one == 0) | (two == 0), 0.0, -1e30)
            high = jnp.where((one == 1) | (two == 1), 0.0, -1e30)
            bias = jnp.where(first_half, low, high)
            scale = jnp.where(k < amount, inv_root, 0.0)
            items += [(rows, place, bias, scale, h) for h in range(heads)]
        q = [q_ref[rows, key_cols[h]] for rows, _, _, _, h in items]
        scores = [
            dot(x, kv[place, :, key_cols[h]], NT) * (inv_root * math.log2(math.e)) + bias
            for x, (_, place, bias, _, h) in zip(q, items)
        ]
        grad_probs = [
            dot(cot_ref[rows, key_cols[h]], kv[place, :, value_cols[h]], NT)
            for rows, place, _, _, h in items
        ]
        highest = [jnp.max(s, axis=1, keepdims=True) for s in scores]
        weights = [jnp.exp2(s - m) for s, m in zip(scores, highest)]
        sums = [jnp.sum(w, axis=1, keepdims=True) for w in weights]
        probs = [w * (1.0 / s) for w, s in zip(weights, sums)]
        deltas = [jnp.sum(p * g, axis=1, keepdims=True) for p, g in zip(probs, grad_probs)]
        grad_scores = [
            (p * (g - d) * item[3]).astype(jnp.bfloat16)
            for p, g, d, item in zip(probs, grad_probs, deltas, items)
        ]
        for p, (rows, place, _, _, h) in zip(probs, items):
            att = jnp.dot(
                p.astype(jnp.bfloat16),
                kv[place, :, value_cols[h]],
                preferred_element_type=jnp.float32,
            )
            att_ref[rows, key_cols[h]] = att.astype(jnp.bfloat16)
        for x, g, (_, place, _, _, h) in zip(q, grad_scores, items):
            acc[place, key_cols[h]] += dot(x, g, TN)
        return carry

    lax.fori_loop(0, (amount + TOGETHER - 1) // TOGETHER, step, 0)

    start = 0
    for ref, size in zip(grad_refs, sizes):

        def round_block(b, carry, ref=ref, start=start):
            ref[b] = acc[start + b].astype(jnp.bfloat16)
            return carry

        lax.fori_loop(0, size, round_block, 0)
        start += size


def attend(work, ids, q, cot, column, parts, earlier=None):
    seen, width = parts[0].shape[1], parts[0].shape[2] // 2
    heads, tokens = width // D_HEAD, q.shape[0]
    sizes = [part.shape[0] for part in parts]
    whole = pl.BlockSpec((tokens, width), lambda i, *_: (0, 0))
    chunk = pl.BlockSpec((tokens, width), lambda i, *_: (0, column))
    before = [] if earlier is None else [earlier]
    out = pl.pallas_call(
        functools.partial(attention_kernel, heads, sizes, bool(before)),
        grid_spec=pltpu.PrefetchScalarGridSpec(
            num_scalar_prefetch=4,
            grid=(1,),
            in_specs=[chunk, chunk]
            + [pl.BlockSpec(memory_space=pl.ANY)] * len(parts)
            + [whole] * len(before),
            out_specs=[whole]
            + [pl.BlockSpec((size, width, seen), lambda i, *_: (0, 0, 0)) for size in sizes],
            scratch_shapes=[
                pltpu.VMEM((sum(sizes), seen, 2 * width), jnp.bfloat16),
                pltpu.VMEM((sum(sizes), width, seen), jnp.float32),
                pltpu.SemaphoreType.DMA((len(sizes),)),
            ],
        ),
        out_shape=[jax.ShapeDtypeStruct((tokens, width), jnp.bfloat16)]
        + [jax.ShapeDtypeStruct((size, width, seen), jnp.bfloat16) for size in sizes],
        compiler_params=pltpu.CompilerParams(vmem_limit_bytes=48 * 1024 * 1024),
        cost_estimate=pl.CostEstimate(
            flops=tokens * seen * width * 4,
            bytes_accessed=sum(sizes) * seen * width * 6 + tokens * width * 6,
            transcendentals=tokens * seen * heads,
        ),
    )(*work, ids, q, cot, *parts, *before)
    return out[0], list(out[1:])


def normed_store(database, norm_gain):
    rows = database.reshape(-1, database.shape[2])
    stored = rows.shape[0]
    top = lax.reduce_precision(norm_gain, 8, 7)
    middle = lax.reduce_precision(norm_gain - top, 8, 7)
    bottom = norm_gain - top - middle
    gains = jnp.stack([top, middle, bottom]).astype(jnp.bfloat16)
    packed = jnp.concatenate([rows, jnp.pad(gains, ((0, 13), (0, 0)))], axis=0)
    whole = lax.all_gather(packed, "tp", axis=1, tiled=True).astype(jnp.float32)
    floats = whole[:stored]
    gain = whole[stored] + whole[stored + 1] + whole[stored + 2]
    mean = jnp.sum(floats * floats, axis=1, keepdims=True) / floats.shape[1]
    return (floats * lax.rsqrt(mean + epsilon) * gain[None, :]).astype(jnp.bfloat16)


def core_rows(x, core):
    return lax.dynamic_index_in_dim(x.reshape(x.shape[0], CHIPS, 2, -1), core, 2, False)


def scatter_gradient(total, rows):
    width = total.shape[1]
    for groups in (Y_GROUPS, Z_GROUPS):
        size = len(groups[0])
        total = total.astype(jnp.bfloat16).reshape(size, -1, rows, width)
        total = lax.all_to_all(total, "seq", 0, 0, axis_index_groups=groups, tiled=True)
        total = jnp.sum(total.astype(jnp.float32), axis=0)
    return total.reshape(rows, width)


def per_device(
    queries, cotangent, owner_map, neighbour_ids, database, norm_gain, key_weight, value_weight
):
    core = lax.axis_index("seq") % 2
    tokens, local_width = queries.shape
    width = local_width // 2

    meta = jnp.concatenate([owner_map, neighbour_ids], axis=1)
    meta = jnp.concatenate([meta, swap(meta)], axis=0)
    q = jnp.concatenate([queries, swap(queries)], axis=0)
    cot = jnp.concatenate([cotangent, swap(cotangent)], axis=0)
    owners, ids = meta[:, 0], meta[:, 1:].reshape(-1)
    chip = lax.axis_index("seq") // 2
    member = owners % 2 == core
    y_place = ring_place(owners // (2 * N_Z) - chip // N_Z, N_Y)
    z_place = ring_place(owners // 2 - chip, N_Z)

    normed = normed_store(database, norm_gain)
    key_rows = jnp.dot(normed, key_weight, preferred_element_type=jnp.float32).astype(jnp.bfloat16)
    value_rows = jnp.dot(normed, value_weight, preferred_element_type=jnp.float32).astype(
        jnp.bfloat16
    )

    chip_normed = [core_rows(normed, core), swap(core_rows(normed, 1 - core))]
    chip_normed = jnp.concatenate(chip_normed, axis=0).reshape(2 * normed.shape[0], -1)

    kv = [
        jnp.concatenate([r[:, i * width : (i + 1) * width] for r in (key_rows, value_rows)], axis=1)
        for i in range(2)
    ]

    place_one = y_place * N_Z + z_place
    place_two = z_place * N_Y + y_place
    work_one = functools.partial(work_list, place_one, member)
    work_two = functools.partial(work_list, place_two, member)

    with jax.named_scope("one"):
        line_one = join(ring_gather(kv[0], from_z, N_Z))
        one = ring_near(line_one, from_y, N_Y)
    with jax.named_scope("two"):
        line_two = join(ring_gather(kv[1], from_y, N_Y))
        two = ring_near(line_two, from_z, N_Z)
    with jax.named_scope("two_near"):
        att_two, grads_two = attend(work_two(0, 5 * N_Y), ids, q, cot, 1, two[:5])
    with jax.named_scope("two"):
        two[-2:] = after(two[-2:], att_two)
        two += ring_far(two, from_z)
    with jax.named_scope("one"):
        one[-2:] = after(one[-2:], att_two)
        one += ring_far(one, from_y)
    with jax.named_scope("one_near"):
        att_one, grads_one = attend(work_one(0, 3 * N_Z), ids, q, cot, 0, one[:3])
    with jax.named_scope("two_far"):
        att_two, more = attend(
            work_two(5 * N_Y, CHIPS), ids, q, cot, 1, two[5:], after(att_two, att_one)
        )
        grads_two += more
    with jax.named_scope("one_far"):
        att_one, more = attend(
            work_one(3 * N_Z, CHIPS), ids, q, cot, 0, one[3:], after(att_one, att_two)
        )
        grads_one += more

    with jax.named_scope("two"):
        sums = ring_scatter(grads_two, from_z, N_Z)
        grad_two = ring_scatter([*sums[:-1], *halves(sums[-1])], from_y, N_Y)
    with jax.named_scope("one"):
        sums = ring_scatter(grads_one, from_y, N_Y)
        grad_one = ring_scatter([*sums[:-1], *halves(sums[-1])], from_z, N_Z)

    here = owner_map % 2 == core
    here = jnp.broadcast_to(here, (here.shape[0], SPAN)).reshape(tokens, 1)
    attended = [jnp.where(here, att[:tokens], swap(att[tokens:])) for att in (att_one, att_two)]
    grad_keys = jnp.concatenate([grad_one, grad_two], axis=0)
    grad_keys = jnp.concatenate([grad_keys, swap(grad_keys)], axis=1)
    grad = lax.dot_general(
        chip_normed, grad_keys, (((0,), (1,)), ((), ())), preferred_element_type=jnp.float32
    )
    return jnp.concatenate(attended, axis=1), scatter_gradient(grad, normed.shape[1] // (2 * CHIPS))


def solution(mesh):
    placed = (
        P("seq", "tp"),
        P("seq", "tp"),
        P("seq", None),
        P("seq", None),
        P("seq", None, "tp"),
        P("tp"),
        P(None, "tp"),
        P(None, "tp"),
    )
    return jax.shard_map(
        per_device,
        mesh=mesh,
        in_specs=placed,
        out_specs=(P("seq", "tp"), P("seq", "tp")),
        check_vma=False,
    )
```

```python
import functools
import math

import jax
import jax.numpy as jnp
from jax import lax
from jax.experimental import pallas as pl
from jax.experimental.pallas import tpu as pltpu
from jax.sharding import PartitionSpec as P

D_HEAD = 128
SPAN = 64
NLEN = 128
N_Y, N_Z = 4, 8
CHIPS = N_Y * N_Z
TOGETHER = 2
epsilon = 1e-06


def seq_of(y, z, core):
    return ((y % N_Y) * N_Z + z % N_Z) * 2 + core


PAIR = [(i, i ^ 1) for i in range(2 * CHIPS)]
Z_GROUPS = [[seq_of(y, z, c) for z in range(N_Z)] for y in range(N_Y) for c in range(2)]
Y_GROUPS = [[seq_of(y, z, c) for y in range(N_Y)] for z in range(N_Z) for c in range(2)]
LINES = [[seq_of(y, z, c) for y in range(N_Y) for c in range(2)] for z in range(N_Z)]
CELLS = [(y, z, c) for y in range(N_Y) for z in range(N_Z) for c in range(2)]
NT = (((1,), (1,)), ((), ()))
TN = (((0,), (0,)), ((), ()))


def swap(x):
    with jax.named_scope("swap"):
        return lax.ppermute(x, "seq", PAIR)


def from_y(x, step):
    with jax.named_scope("y"):
        return lax.ppermute(x, "seq", [(seq_of(y + step, z, c), seq_of(y, z, c)) for y, z, c in CELLS])


def from_z(x, step):
    with jax.named_scope("z"):
        return lax.ppermute(x, "seq", [(seq_of(y, z + step, c), seq_of(y, z, c)) for y, z, c in CELLS])


def add(x, *others):
    total = x.astype(jnp.float32)
    for other in others:
        total = total + other.astype(jnp.float32)
    return total.astype(jnp.bfloat16)


def after(values, done):
    return lax.optimization_barrier((values, done))[0]


def halves(x):
    middle = x.shape[0] // 2
    return x[:middle], x[middle:]


def ring_near(x, fetch, size):
    up, down, parts = x, x, [x]
    for hop in range(1, size // 2):
        with jax.named_scope(f"gather_{hop}"):
            up, down = fetch(up, 1), fetch(down, -1)
        parts += [up, down]
    return parts


def ring_far(parts, fetch):
    with jax.named_scope("gather_far"):
        return [fetch(halves(parts[-2])[0], 1), fetch(halves(parts[-1])[1], -1)]


def ring_scatter(parts, fetch, size):
    plus, minus = parts[size - 3], parts[size - 2]
    with jax.named_scope("scatter_far"):
        if len(parts) == size:
            plus = add(plus, fetch(parts[-1], -1))
        else:
            first, second = fetch(parts[-2], -1), fetch(parts[-1], 1)
            plus = jnp.concatenate([add(halves(plus)[0], first), halves(plus)[1]])
            minus = jnp.concatenate([halves(minus)[0], add(halves(minus)[1], second)])
    for hop in range(size // 2 - 2, 0, -1):
        with jax.named_scope(f"scatter_{hop + 1}"):
            plus, minus = (
                add(parts[2 * hop - 1], fetch(plus, -1)),
                add(parts[2 * hop], fetch(minus, 1)),
            )
    with jax.named_scope("scatter_1"):
        return add(parts[0], fetch(plus, -1), fetch(minus, 1))


def ring_place(offset, size):
    offset = offset % size
    place = jnp.where(offset < size // 2, 2 * offset - 1, 2 * (size - offset))
    place = jnp.where(offset == size // 2, size - 1, place)
    return jnp.where(offset == 0, 0, place)


def work_list(place, chosen):
    order = jnp.arange(place.shape[0])
    before = order[None, :] < order[:, None]
    rank = jnp.sum((before & chosen[None, :]).astype(jnp.int32), axis=1)
    at = chosen[None, :] & (rank[None, :] == order[:, None])
    listed = jnp.sum(jnp.where(at, order[None, :], 0), axis=1).astype(jnp.int32)
    block = jnp.sum(jnp.where(at, place[None, :], 0), axis=1).astype(jnp.int32)
    return jnp.sum(chosen.astype(jnp.int32)).reshape(1), listed, block


def attention_kernel(heads, last, number, listed, block, ids, spans, *refs):
    taken = N_Z + 1 + last
    sources, refs = refs[:taken], refs[taken:]
    qc, kv, acc, att, semaphores = refs[-5:]
    out, grad_outs = refs[0], refs[1:-5]
    inv_root = 1.0 / math.sqrt(D_HEAD)
    dot = functools.partial(lax.dot_general, preferred_element_type=jnp.float32)
    devices, tokens = out.shape[:2]

    moves = [
        (spans.at[i, pl.ds(j * tokens, tokens)], qc.at[j, pl.ds(i * tokens, tokens)])
        for i in range(devices)
        for j in range(2)
    ]
    for i, source in enumerate(sources[: N_Z - 1]):
        moves.append((source, kv.at[i]))
    for i, source in enumerate(sources[N_Z - 1 : N_Z + 1]):
        moves.append((source, kv.at[N_Z - 1, pl.ds(i * NLEN, NLEN)]))
    if last:
        moves.append((sources[-1], acc))
    copies = [
        pltpu.make_async_copy(source, target, semaphores.at[i])
        for i, (source, target) in enumerate(moves)
    ]
    for copy in copies:
        copy.start()
    if not last:
        acc[...] = jnp.zeros_like(acc)
    att[...] = jnp.zeros_like(att)
    for copy in copies:
        copy.wait()

    first_half = lax.broadcasted_iota(jnp.int32, (1, 2 * NLEN), 1) < NLEN
    amount = number[0]
    width = heads * D_HEAD
    key_cols = [slice(h * D_HEAD, (h + 1) * D_HEAD) for h in range(heads)]
    value_cols = [slice(width + h * D_HEAD, width + (h + 1) * D_HEAD) for h in range(heads)]

    def step(i, carry):
        items = []
        for u in range(TOGETHER):
            k = i * TOGETHER + u
            at = jnp.minimum(k, amount - 1)
            span, place = listed[at], block[at]
            rows = pl.ds(pl.multiple_of(span * SPAN, SPAN), SPAN)
            one, two = ids[2 * span], ids[2 * span + 1]
            low = jnp.where((one == 0) | (two == 0), 0.0, -1e30)
            high = jnp.where((one == 1) | (two == 1), 0.0, -1e30)
            bias = jnp.where(first_half, low, high)
            scale = jnp.where(k < amount, inv_root, 0.0)
            items += [(rows, place, bias, scale, h) for h in range(heads)]
        q = [qc[0, rows, key_cols[h]] for rows, _, _, _, h in items]
        scores = [
            dot(x, kv[place, :, key_cols[h]], NT) * (inv_root * math.log2(math.e)) + bias
            for x, (_, place, bias, _, h) in zip(q, items)
        ]
        grad_probs = [
            dot(qc[1, rows, key_cols[h]], kv[place, :, value_cols[h]], NT)
            for rows, place, _, _, h in items
        ]
        highest = [jnp.max(s, axis=1, keepdims=True) for s in scores]
        weights = [jnp.exp2(s - m) for s, m in zip(scores, highest)]
        sums = [jnp.sum(w, axis=1, keepdims=True) for w in weights]
        probs = [w * (1.0 / s) for w, s in zip(weights, sums)]
        deltas = [jnp.sum(p * g, axis=1, keepdims=True) for p, g in zip(probs, grad_probs)]
        grad_scores = [
            (p * (g - d) * item[3]).astype(jnp.bfloat16)
            for p, g, d, item in zip(probs, grad_probs, deltas, items)
        ]
        for p, (rows, place, _, _, h) in zip(probs, items):
            out = jnp.dot(
                p.astype(jnp.bfloat16),
                kv[place, :, value_cols[h]],
                preferred_element_type=jnp.float32,
            )
            att[rows, key_cols[h]] = out.astype(jnp.bfloat16)
        for x, g, (_, place, _, _, h) in zip(q, grad_scores, items):
            acc[place, key_cols[h]] += dot(x, g, TN)
        return carry

    lax.fori_loop(0, (amount + TOGETHER - 1) // TOGETHER, step, 0)

    copies = [
        pltpu.make_async_copy(att.at[pl.ds(i * tokens, tokens)], out.at[i], semaphores.at[i])
        for i in range(devices)
    ]
    if not last:
        copies.append(pltpu.make_async_copy(acc, grad_outs[0], semaphores.at[devices]))
    for copy in copies:
        copy.start()
    if last:
        for i, ref in enumerate(grad_outs[: N_Z - 1]):
            ref[...] = acc[i].astype(jnp.bfloat16)
        for i, ref in enumerate(grad_outs[N_Z - 1 :]):
            ref[...] = acc[N_Z - 1, i * width // 2 : (i + 1) * width // 2].astype(jnp.bfloat16)
    for copy in copies:
        copy.wait()


def attend(work, ids, spans, tokens, parts, earlier=None):
    seen, width = parts[0].shape[0], parts[0].shape[1] // 2
    heads, last, devices = width // D_HEAD, earlier is not None, spans.shape[0]
    rows = devices * tokens
    operands = [spans, *parts] + ([earlier] if last else [])
    anywhere = pl.BlockSpec(memory_space=pl.ANY)
    sums = jax.ShapeDtypeStruct((N_Z, width, seen), jnp.float32)
    shapes = [(width, seen)] * (N_Z - 1) + [(width // 2, seen)] * 2
    out = pl.pallas_call(
        functools.partial(attention_kernel, heads, last),
        grid_spec=pltpu.PrefetchScalarGridSpec(
            num_scalar_prefetch=4,
            grid=(1,),
            in_specs=[anywhere] * len(operands),
            out_specs=[anywhere]
            + ([pl.BlockSpec(shape, lambda i, *_: (0, 0)) for shape in shapes] if last else [anywhere]),
            scratch_shapes=[
                pltpu.VMEM((2, rows, width), jnp.bfloat16),
                pltpu.VMEM((N_Z, seen, 2 * width), jnp.bfloat16),
                pltpu.VMEM((N_Z, width, seen), jnp.float32),
                pltpu.VMEM((rows, width), jnp.bfloat16),
                pltpu.SemaphoreType.DMA((2 * devices + N_Z + 2,)),
            ],
        ),
        out_shape=[jax.ShapeDtypeStruct((devices, tokens, width), jnp.bfloat16)]
        + ([jax.ShapeDtypeStruct(shape, jnp.bfloat16) for shape in shapes] if last else [sums]),
        compiler_params=pltpu.CompilerParams(vmem_limit_bytes=50 * 1024 * 1024),
        cost_estimate=pl.CostEstimate(
            flops=rows * seen * width * 2,
            bytes_accessed=rows * width * 6 + N_Z * seen * width * 10,
            transcendentals=rows * seen * heads // 4,
        ),
    )(*work, ids, *operands)
    return out[0], list(out[1:])


def normed_store(database, norm_gain):
    rows = database.reshape(-1, database.shape[2])
    stored = rows.shape[0]
    top = lax.reduce_precision(norm_gain, 8, 7)
    middle = lax.reduce_precision(norm_gain - top, 8, 7)
    bottom = norm_gain - top - middle
    gains = jnp.stack([top, middle, bottom]).astype(jnp.bfloat16)
    packed = jnp.concatenate([rows, jnp.pad(gains, ((0, 13), (0, 0)))], axis=0)
    whole = lax.all_gather(packed, "tp", axis=1, tiled=True).astype(jnp.float32)
    floats = whole[:stored]
    gain = whole[stored] + whole[stored + 1] + whole[stored + 2]
    mean = jnp.sum(floats * floats, axis=1, keepdims=True) / floats.shape[1]
    return (floats * lax.rsqrt(mean + epsilon) * gain[None, :]).astype(jnp.bfloat16)


def core_rows(x, core):
    return lax.dynamic_index_in_dim(x.reshape(x.shape[0], CHIPS, 2, -1), core, 2, False)


def scatter_gradient(total, rows):
    width = total.shape[1]
    for groups in (Y_GROUPS, Z_GROUPS):
        size = len(groups[0])
        total = total.astype(jnp.bfloat16).reshape(size, -1, rows, width)
        total = lax.all_to_all(total, "seq", 0, 0, axis_index_groups=groups, tiled=True)
        total = jnp.sum(total.astype(jnp.float32), axis=0)
    return total.reshape(rows, width)


def per_device(
    queries, cotangent, owner_map, neighbour_ids, database, norm_gain, key_weight, value_weight
):
    index = lax.axis_index("seq")
    core, here_y, here_z = index % 2, index // (2 * N_Z), index // 2 % N_Z
    tokens, local_width = queries.shape

    half = tokens // 2
    with jax.named_scope("spans"):
        meta = jnp.concatenate([owner_map, neighbour_ids], axis=1).T.astype(jnp.bfloat16)
        meta = meta.reshape(3, 2, -1)
        meta = jnp.pad(meta, ((0, 13), (0, 0), (0, local_width - meta.shape[2])))
        lines = []
        for i in range(2):
            rows = slice(i * half, (i + 1) * half)
            line = jnp.concatenate([queries[rows], cotangent[rows], meta[:, i]], axis=0)
            lines.append(lax.all_gather(line, "seq", axis_index_groups=LINES, axis=0, tiled=False))

    normed = normed_store(database, norm_gain)
    key_rows = jnp.dot(normed, key_weight, preferred_element_type=jnp.float32).astype(jnp.bfloat16)
    value_rows = jnp.dot(normed, value_weight, preferred_element_type=jnp.float32).astype(
        jnp.bfloat16
    )

    chip_normed = [core_rows(normed, core), swap(core_rows(normed, 1 - core))]
    chip_normed = jnp.concatenate(chip_normed, axis=0).reshape(2 * normed.shape[0], -1)

    with jax.named_scope("keys_values"):
        kv = jnp.concatenate([key_rows, value_rows], axis=1)
        kv = ring_near(kv, from_z, N_Z)
        kv += ring_far(kv, from_z)

    sums, attended = None, []
    for line in lines:
        if sums is not None:
            line = after(line, sums[0])
        meta = line[:, tokens : tokens + 3, : half // SPAN].astype(jnp.int32)
        owners, ids = meta[:, 0].reshape(-1), meta[:, 1:].transpose(0, 2, 1).reshape(-1)
        member = (owners % 2 == core) & (owners // (2 * N_Z) == here_y)
        work = work_list(ring_place(owners // 2 - here_z, N_Z), member)
        with jax.named_scope("attend"):
            att, sums = attend(work, ids, line, half, kv, None if sums is None else sums[0])
        with jax.named_scope("attended"):
            attended.append(
                lax.psum_scatter(att, "seq", axis_index_groups=LINES, scatter_dimension=0, tiled=False)
            )
    with jax.named_scope("key_gradients"):
        grad_keys = ring_scatter(sums, from_z, N_Z)

    grad_keys = jnp.concatenate([grad_keys, swap(grad_keys)], axis=1)
    grad = lax.dot_general(
        chip_normed, grad_keys, (((0,), (1,)), ((), ())), preferred_element_type=jnp.float32
    )
    grad = scatter_gradient(grad, normed.shape[1] // (2 * CHIPS))
    return jnp.concatenate(attended, axis=0), grad


def solution(mesh):
    placed = (
        P("seq", "tp"),
        P("seq", "tp"),
        P("seq", None),
        P("seq", None),
        P("seq", None, "tp"),
        P("tp"),
        P(None, "tp"),
        P(None, "tp"),
    )
    return jax.shard_map(
        per_device,
        mesh=mesh,
        in_specs=placed,
        out_specs=(P("seq", "tp"), P("seq", "tp")),
        check_vma=False,
    )
```

```python
import functools
import math

import jax
import jax.numpy as jnp
from jax import lax
from jax.experimental import pallas as pl
from jax.experimental.pallas import tpu as pltpu
from jax.sharding import PartitionSpec as P

D_HEAD = 128
SPAN = 64
NLEN = 128
N_Y, N_Z = 4, 8
CHIPS = N_Y * N_Z
TOGETHER = 2
epsilon = 1e-06


def seq_of(y, z, core):
    return ((y % N_Y) * N_Z + z % N_Z) * 2 + core


PAIR = [(i, i ^ 1) for i in range(2 * CHIPS)]
Z_GROUPS = [[seq_of(y, z, c) for z in range(N_Z)] for y in range(N_Y) for c in range(2)]
Y_GROUPS = [[seq_of(y, z, c) for y in range(N_Y)] for z in range(N_Z) for c in range(2)]
LINES = [[seq_of(y, z, c) for y in range(N_Y) for c in range(2)] for z in range(N_Z)]
CELLS = [(y, z, c) for y in range(N_Y) for z in range(N_Z) for c in range(2)]
NT = (((1,), (1,)), ((), ()))
TN = (((0,), (0,)), ((), ()))


def swap(x):
    with jax.named_scope("swap"):
        return lax.ppermute(x, "seq", PAIR)


def from_y(x, step):
    with jax.named_scope("y"):
        return lax.ppermute(x, "seq", [(seq_of(y + step, z, c), seq_of(y, z, c)) for y, z, c in CELLS])


def from_z(x, step):
    with jax.named_scope("z"):
        return lax.ppermute(x, "seq", [(seq_of(y, z + step, c), seq_of(y, z, c)) for y, z, c in CELLS])


def add(x, *others):
    total = x.astype(jnp.float32)
    for other in others:
        total = total + other.astype(jnp.float32)
    return total.astype(jnp.bfloat16)


def after(values, done):
    return lax.optimization_barrier((values, done))[0]


def halves(x):
    middle = x.shape[0] // 2
    return x[:middle], x[middle:]


def ring_near(x, fetch, size):
    up, down, parts = x, x, [x]
    for hop in range(1, size // 2):
        with jax.named_scope(f"gather_{hop}"):
            up, down = fetch(up, 1), fetch(down, -1)
        parts += [up, down]
    return parts


def ring_far(parts, fetch):
    with jax.named_scope("gather_far"):
        return [fetch(halves(parts[-2])[0], 1), fetch(halves(parts[-1])[1], -1)]


def ring_scatter(parts, fetch, size):
    plus, minus = parts[size - 3], parts[size - 2]
    with jax.named_scope("scatter_far"):
        if len(parts) == size:
            plus = add(plus, fetch(parts[-1], -1))
        else:
            first, second = fetch(parts[-2], -1), fetch(parts[-1], 1)
            plus = jnp.concatenate([add(halves(plus)[0], first), halves(plus)[1]])
            minus = jnp.concatenate([halves(minus)[0], add(halves(minus)[1], second)])
    for hop in range(size // 2 - 2, 0, -1):
        with jax.named_scope(f"scatter_{hop + 1}"):
            plus, minus = (
                add(parts[2 * hop - 1], fetch(plus, -1)),
                add(parts[2 * hop], fetch(minus, 1)),
            )
    with jax.named_scope("scatter_1"):
        return add(parts[0], fetch(plus, -1), fetch(minus, 1))


def ring_place(offset, size):
    offset = offset % size
    place = jnp.where(offset < size // 2, 2 * offset - 1, 2 * (size - offset))
    place = jnp.where(offset == size // 2, size - 1, place)
    return jnp.where(offset == 0, 0, place)


def work_list(place, chosen):
    order = jnp.arange(place.shape[0])
    before = order[None, :] < order[:, None]
    rank = jnp.sum((before & chosen[None, :]).astype(jnp.int32), axis=1)
    at = chosen[None, :] & (rank[None, :] == order[:, None])
    listed = jnp.sum(jnp.where(at, order[None, :], 0), axis=1).astype(jnp.int32)
    block = jnp.sum(jnp.where(at, place[None, :], 0), axis=1).astype(jnp.int32)
    return jnp.sum(chosen.astype(jnp.int32)).reshape(1), listed, block


def attention_kernel(heads, last, number, listed, block, ids, spans, *refs):
    taken = N_Z + 1 + last
    sources, refs = refs[:taken], refs[taken:]
    qc, kv, acc, att, semaphores = refs[-5:]
    out, grad_outs = refs[0], refs[1:-5]
    inv_root = 1.0 / math.sqrt(D_HEAD)
    dot = functools.partial(lax.dot_general, preferred_element_type=jnp.float32)
    devices, tokens = out.shape[:2]

    moves = [
        (spans.at[i, pl.ds(j * tokens, tokens)], qc.at[j, pl.ds(i * tokens, tokens)])
        for i in range(devices)
        for j in range(2)
    ]
    for i, source in enumerate(sources[: N_Z - 1]):
        moves.append((source, kv.at[i]))
    for i, source in enumerate(sources[N_Z - 1 : N_Z + 1]):
        moves.append((source, kv.at[N_Z - 1, pl.ds(i * NLEN, NLEN)]))
    if last:
        moves.append((sources[-1], acc))
    copies = [
        pltpu.make_async_copy(source, target, semaphores.at[i])
        for i, (source, target) in enumerate(moves)
    ]
    for copy in copies:
        copy.start()
    if not last:
        acc[...] = jnp.zeros_like(acc)
    att[...] = jnp.zeros_like(att)
    for copy in copies:
        copy.wait()

    first_half = lax.broadcasted_iota(jnp.int32, (1, 2 * NLEN), 1) < NLEN
    amount = number[0]
    width = heads * D_HEAD
    key_cols = [slice(h * D_HEAD, (h + 1) * D_HEAD) for h in range(heads)]
    value_cols = [slice(width + h * D_HEAD, width + (h + 1) * D_HEAD) for h in range(heads)]

    def step(i, carry):
        items = []
        for u in range(TOGETHER):
            k = i * TOGETHER + u
            at = jnp.minimum(k, amount - 1)
            span, place = listed[at], block[at]
            rows = pl.ds(pl.multiple_of(span * SPAN, SPAN), SPAN)
            one, two = ids[2 * span], ids[2 * span + 1]
            low = jnp.where((one == 0) | (two == 0), 0.0, -1e30)
            high = jnp.where((one == 1) | (two == 1), 0.0, -1e30)
            bias = jnp.where(first_half, low, high)
            scale = jnp.where(k < amount, inv_root, 0.0)
            items += [(rows, place, bias, scale, h) for h in range(heads)]
        q = [qc[0, rows, key_cols[h]] for rows, _, _, _, h in items]
        scores = [
            dot(x, kv[place, :, key_cols[h]], NT) * (inv_root * math.log2(math.e)) + bias
            for x, (_, place, bias, _, h) in zip(q, items)
        ]
        grad_probs = [
            dot(qc[1, rows, key_cols[h]], kv[place, :, value_cols[h]], NT)
            for rows, place, _, _, h in items
        ]
        highest = [jnp.max(s, axis=1, keepdims=True) for s in scores]
        weights = [jnp.exp2(s - m) for s, m in zip(scores, highest)]
        sums = [jnp.sum(w, axis=1, keepdims=True) for w in weights]
        probs = [w * (1.0 / s) for w, s in zip(weights, sums)]
        deltas = [jnp.sum(p * g, axis=1, keepdims=True) for p, g in zip(probs, grad_probs)]
        grad_scores = [
            (p * (g - d) * item[3]).astype(jnp.bfloat16)
            for p, g, d, item in zip(probs, grad_probs, deltas, items)
        ]
        for p, (rows, place, _, _, h) in zip(probs, items):
            out = jnp.dot(
                p.astype(jnp.bfloat16),
                kv[place, :, value_cols[h]],
                preferred_element_type=jnp.float32,
            )
            att[rows, key_cols[h]] = out.astype(jnp.bfloat16)
        for x, g, (_, place, _, _, h) in zip(q, grad_scores, items):
            acc[place, key_cols[h]] += dot(x, g, TN)
        return carry

    lax.fori_loop(0, (amount + TOGETHER - 1) // TOGETHER, step, 0)

    copies = [
        pltpu.make_async_copy(att.at[pl.ds(i * tokens, tokens)], out.at[i], semaphores.at[i])
        for i in range(devices)
    ]
    if not last:
        copies.append(pltpu.make_async_copy(acc, grad_outs[0], semaphores.at[devices]))
    for copy in copies:
        copy.start()
    if last:
        for i, ref in enumerate(grad_outs[: N_Z - 1]):
            ref[...] = acc[i].astype(jnp.bfloat16)
        for i, ref in enumerate(grad_outs[N_Z - 1 :]):
            ref[...] = acc[N_Z - 1, i * width // 2 : (i + 1) * width // 2].astype(jnp.bfloat16)
    for copy in copies:
        copy.wait()


def attend(work, ids, spans, tokens, parts, earlier=None):
    seen, width = parts[0].shape[0], parts[0].shape[1] // 2
    heads, last, devices = width // D_HEAD, earlier is not None, spans.shape[0]
    rows = devices * tokens
    operands = [spans, *parts] + ([earlier] if last else [])
    anywhere = pl.BlockSpec(memory_space=pl.ANY)
    sums = jax.ShapeDtypeStruct((N_Z, width, seen), jnp.float32)
    shapes = [(width, seen)] * (N_Z - 1) + [(width // 2, seen)] * 2
    out = pl.pallas_call(
        functools.partial(attention_kernel, heads, last),
        grid_spec=pltpu.PrefetchScalarGridSpec(
            num_scalar_prefetch=4,
            grid=(1,),
            in_specs=[anywhere] * len(operands),
            out_specs=[anywhere]
            + ([pl.BlockSpec(shape, lambda i, *_: (0, 0)) for shape in shapes] if last else [anywhere]),
            scratch_shapes=[
                pltpu.VMEM((2, rows, width), jnp.bfloat16),
                pltpu.VMEM((N_Z, seen, 2 * width), jnp.bfloat16),
                pltpu.VMEM((N_Z, width, seen), jnp.float32),
                pltpu.VMEM((rows, width), jnp.bfloat16),
                pltpu.SemaphoreType.DMA((2 * devices + N_Z + 2,)),
            ],
        ),
        out_shape=[jax.ShapeDtypeStruct((devices, tokens, width), jnp.bfloat16)]
        + ([jax.ShapeDtypeStruct(shape, jnp.bfloat16) for shape in shapes] if last else [sums]),
        compiler_params=pltpu.CompilerParams(vmem_limit_bytes=50 * 1024 * 1024),
        cost_estimate=pl.CostEstimate(
            flops=rows * seen * width * 2,
            bytes_accessed=rows * width * 6 + N_Z * seen * width * 10,
            transcendentals=rows * seen * heads // 4,
        ),
    )(*work, ids, *operands)
    return out[0], list(out[1:])


def normed_store(database, norm_gain):
    rows = database.reshape(-1, database.shape[2])
    stored = rows.shape[0]
    top = lax.reduce_precision(norm_gain, 8, 7)
    middle = lax.reduce_precision(norm_gain - top, 8, 7)
    bottom = norm_gain - top - middle
    gains = jnp.stack([top, middle, bottom]).astype(jnp.bfloat16)
    packed = jnp.concatenate([rows, jnp.pad(gains, ((0, 13), (0, 0)))], axis=0)
    whole = lax.all_gather(packed, "tp", axis=1, tiled=True).astype(jnp.float32)
    floats = whole[:stored]
    gain = whole[stored] + whole[stored + 1] + whole[stored + 2]
    mean = jnp.sum(floats * floats, axis=1, keepdims=True) / floats.shape[1]
    return (floats * lax.rsqrt(mean + epsilon) * gain[None, :]).astype(jnp.bfloat16)


def core_rows(x, core):
    return lax.dynamic_index_in_dim(x.reshape(x.shape[0], CHIPS, 2, -1), core, 2, False)


def scatter_gradient(total, rows):
    width = total.shape[1]
    for groups in (Y_GROUPS, Z_GROUPS):
        size = len(groups[0])
        total = total.astype(jnp.bfloat16).reshape(size, -1, rows, width)
        total = lax.all_to_all(total, "seq", 0, 0, axis_index_groups=groups, tiled=True)
        total = jnp.sum(total.astype(jnp.float32), axis=0)
    return total.reshape(rows, width)


def per_device(
    queries, cotangent, owner_map, neighbour_ids, database, norm_gain, key_weight, value_weight
):
    index = lax.axis_index("seq")
    core, here_y, here_z = index % 2, index // (2 * N_Z), index // 2 % N_Z
    tokens, local_width = queries.shape

    half = tokens // 2
    with jax.named_scope("spans"):
        meta = jnp.concatenate([owner_map, neighbour_ids], axis=1).T.astype(jnp.bfloat16)
        meta = meta.reshape(3, 2, -1)
        meta = jnp.pad(meta, ((0, 13), (0, 0), (0, local_width - meta.shape[2])))
        lines = []
        for i in range(2):
            rows = slice(i * half, (i + 1) * half)
            line = jnp.concatenate([queries[rows], cotangent[rows], meta[:, i]], axis=0)
            lines.append(lax.all_gather(line, "seq", axis_index_groups=LINES, axis=0, tiled=False))

    normed = normed_store(database, norm_gain)
    key_rows = jnp.dot(normed, key_weight, preferred_element_type=jnp.float32).astype(jnp.bfloat16)
    value_rows = jnp.dot(normed, value_weight, preferred_element_type=jnp.float32).astype(
        jnp.bfloat16
    )

    chip_normed = [core_rows(normed, core), swap(core_rows(normed, 1 - core))]
    chip_normed = jnp.concatenate(chip_normed, axis=0).reshape(2 * normed.shape[0], -1)

    with jax.named_scope("keys_values"):
        kv = jnp.concatenate([key_rows, value_rows], axis=1)
        kv = ring_near(kv, from_z, N_Z)
        kv += ring_far(kv, from_z)

    sums, attended = None, []
    for line in lines:
        if sums is not None:
            line = after(line, (sums[0], att))
        meta = line[:, tokens : tokens + 3, : half // SPAN].astype(jnp.int32)
        owners, ids = meta[:, 0].reshape(-1), meta[:, 1:].transpose(0, 2, 1).reshape(-1)
        member = (owners % 2 == core) & (owners // (2 * N_Z) == here_y)
        work = work_list(ring_place(owners // 2 - here_z, N_Z), member)
        with jax.named_scope("attend"):
            att, sums = attend(work, ids, line, half, kv, None if sums is None else sums[0])
        with jax.named_scope("attended"):
            groups = LINES
            if not attended:
                att = att.reshape(N_Y, 2, half, local_width)
                ours, theirs = (
                    lax.dynamic_index_in_dim(att, which, 1, False) for which in (core, 1 - core)
                )
                att, groups = ours + swap(theirs), Y_GROUPS
            attended.append(
                lax.psum_scatter(att, "seq", axis_index_groups=groups, scatter_dimension=0, tiled=False)
            )
    with jax.named_scope("key_gradients"):
        grad_keys = ring_scatter(sums, from_z, N_Z)

    grad_keys = jnp.concatenate([grad_keys, swap(grad_keys)], axis=1)
    grad = lax.dot_general(
        chip_normed, grad_keys, (((0,), (1,)), ((), ())), preferred_element_type=jnp.float32
    )
    grad = scatter_gradient(grad, normed.shape[1] // (2 * CHIPS))
    return jnp.concatenate(attended, axis=0), grad


def solution(mesh):
    placed = (
        P("seq", "tp"),
        P("seq", "tp"),
        P("seq", None),
        P("seq", None),
        P("seq", None, "tp"),
        P("tp"),
        P(None, "tp"),
        P(None, "tp"),
    )
    return jax.shard_map(
        per_device,
        mesh=mesh,
        in_specs=placed,
        out_specs=(P("seq", "tp"), P("seq", "tp")),
        check_vma=False,
    )
```

```python
import functools
import math

import jax
import jax.numpy as jnp
from jax import lax
from jax.experimental import pallas as pl
from jax.experimental.pallas import tpu as pltpu
from jax.sharding import PartitionSpec as P

D_HEAD = 128
SPAN = 64
NLEN = 128
N_Y, N_Z = 4, 8
CHIPS = N_Y * N_Z
TOGETHER = 2
epsilon = 1e-06


def seq_of(y, z, core):
    return ((y % N_Y) * N_Z + z % N_Z) * 2 + core


PAIR = [(i, i ^ 1) for i in range(2 * CHIPS)]
Z_GROUPS = [[seq_of(y, z, c) for z in range(N_Z)] for y in range(N_Y) for c in range(2)]
Y_GROUPS = [[seq_of(y, z, c) for y in range(N_Y)] for z in range(N_Z) for c in range(2)]
LINES = [[seq_of(y, z, c) for y in range(N_Y) for c in range(2)] for z in range(N_Z)]
CELLS = [(y, z, c) for y in range(N_Y) for z in range(N_Z) for c in range(2)]
NT = (((1,), (1,)), ((), ()))
TN = (((0,), (0,)), ((), ()))


def swap(x):
    with jax.named_scope("swap"):
        return lax.ppermute(x, "seq", PAIR)


def from_y(x, step):
    with jax.named_scope("y"):
        return lax.ppermute(x, "seq", [(seq_of(y + step, z, c), seq_of(y, z, c)) for y, z, c in CELLS])


def from_z(x, step):
    with jax.named_scope("z"):
        return lax.ppermute(x, "seq", [(seq_of(y, z + step, c), seq_of(y, z, c)) for y, z, c in CELLS])


def add(x, *others):
    total = x.astype(jnp.float32)
    for other in others:
        total = total + other.astype(jnp.float32)
    return total.astype(jnp.bfloat16)


def after(values, done):
    return lax.optimization_barrier((values, done))[0]


def halves(x):
    middle = x.shape[0] // 2
    return x[:middle], x[middle:]


def ring_near(x, fetch, size):
    up, down, parts = x, x, [x]
    for hop in range(1, size // 2):
        with jax.named_scope(f"gather_{hop}"):
            up, down = fetch(up, 1), fetch(down, -1)
        parts += [up, down]
    return parts


def ring_far(parts, fetch):
    with jax.named_scope("gather_far"):
        return [fetch(halves(parts[-2])[0], 1), fetch(halves(parts[-1])[1], -1)]


def ring_scatter(parts, fetch, size):
    plus, minus = parts[size - 3], parts[size - 2]
    with jax.named_scope("scatter_far"):
        if len(parts) == size:
            plus = add(plus, fetch(parts[-1], -1))
        else:
            first, second = fetch(parts[-2], -1), fetch(parts[-1], 1)
            plus = jnp.concatenate([add(halves(plus)[0], first), halves(plus)[1]])
            minus = jnp.concatenate([halves(minus)[0], add(halves(minus)[1], second)])
    for hop in range(size // 2 - 2, 0, -1):
        with jax.named_scope(f"scatter_{hop + 1}"):
            plus, minus = (
                add(parts[2 * hop - 1], fetch(plus, -1)),
                add(parts[2 * hop], fetch(minus, 1)),
            )
    with jax.named_scope("scatter_1"):
        return add(parts[0], fetch(plus, -1), fetch(minus, 1))


def ring_place(offset, size):
    offset = offset % size
    place = jnp.where(offset < size // 2, 2 * offset - 1, 2 * (size - offset))
    place = jnp.where(offset == size // 2, size - 1, place)
    return jnp.where(offset == 0, 0, place)


def work_list(place, chosen):
    order = jnp.arange(place.shape[0])
    before = order[None, :] < order[:, None]
    rank = jnp.sum((before & chosen[None, :]).astype(jnp.int32), axis=1)
    at = chosen[None, :] & (rank[None, :] == order[:, None])
    listed = jnp.sum(jnp.where(at, order[None, :], 0), axis=1).astype(jnp.int32)
    block = jnp.sum(jnp.where(at, place[None, :], 0), axis=1).astype(jnp.int32)
    return jnp.sum(chosen.astype(jnp.int32)).reshape(1), listed, block


def attention_kernel(heads, last, number, listed, block, ids, spans, *refs):
    taken = N_Z + 1 + last
    sources, refs = refs[:taken], refs[taken:]
    qc, kv, acc, att, semaphores = refs[-5:]
    out, grad_outs = refs[0], refs[1:-5]
    inv_root = 1.0 / math.sqrt(D_HEAD)
    dot = functools.partial(lax.dot_general, preferred_element_type=jnp.float32)
    devices, tokens = out.shape[:2]

    moves = [
        (spans.at[i, pl.ds(j * tokens, tokens)], qc.at[j, pl.ds(i * tokens, tokens)])
        for i in range(devices)
        for j in range(2)
    ]
    for i, source in enumerate(sources[: N_Z - 1]):
        moves.append((source, kv.at[i]))
    for i, source in enumerate(sources[N_Z - 1 : N_Z + 1]):
        moves.append((source, kv.at[N_Z - 1, pl.ds(i * NLEN, NLEN)]))
    if last:
        moves.append((sources[-1], acc))
    copies = [
        pltpu.make_async_copy(source, target, semaphores.at[i])
        for i, (source, target) in enumerate(moves)
    ]
    for copy in copies:
        copy.start()
    if not last:
        acc[...] = jnp.zeros_like(acc)
    att[...] = jnp.zeros_like(att)
    for copy in copies:
        copy.wait()

    first_half = lax.broadcasted_iota(jnp.int32, (1, 2 * NLEN), 1) < NLEN
    amount = number[0]
    width = heads * D_HEAD
    key_cols = [slice(h * D_HEAD, (h + 1) * D_HEAD) for h in range(heads)]
    value_cols = [slice(width + h * D_HEAD, width + (h + 1) * D_HEAD) for h in range(heads)]

    def step(i, carry):
        items = []
        for u in range(TOGETHER):
            k = i * TOGETHER + u
            at = jnp.minimum(k, amount - 1)
            span, place = listed[at], block[at]
            rows = pl.ds(pl.multiple_of(span * SPAN, SPAN), SPAN)
            one, two = ids[2 * span], ids[2 * span + 1]
            low = jnp.where((one == 0) | (two == 0), 0.0, -1e30)
            high = jnp.where((one == 1) | (two == 1), 0.0, -1e30)
            bias = jnp.where(first_half, low, high)
            scale = jnp.where(k < amount, inv_root, 0.0)
            items += [(rows, place, bias, scale, h) for h in range(heads)]
        q = [qc[0, rows, key_cols[h]] for rows, _, _, _, h in items]
        scores = [
            dot(x, kv[place, :, key_cols[h]], NT) * (inv_root * math.log2(math.e)) + bias
            for x, (_, place, bias, _, h) in zip(q, items)
        ]
        grad_probs = [
            dot(qc[1, rows, key_cols[h]], kv[place, :, value_cols[h]], NT)
            for rows, place, _, _, h in items
        ]
        highest = [jnp.max(s, axis=1, keepdims=True) for s in scores]
        weights = [jnp.exp2(s - m) for s, m in zip(scores, highest)]
        sums = [jnp.sum(w, axis=1, keepdims=True) for w in weights]
        probs = [w * (1.0 / s) for w, s in zip(weights, sums)]
        deltas = [jnp.sum(p * g, axis=1, keepdims=True) for p, g in zip(probs, grad_probs)]
        grad_scores = [
            (p * (g - d) * item[3]).astype(jnp.bfloat16)
            for p, g, d, item in zip(probs, grad_probs, deltas, items)
        ]
        for p, (rows, place, _, _, h) in zip(probs, items):
            out = jnp.dot(
                p.astype(jnp.bfloat16),
                kv[place, :, value_cols[h]],
                preferred_element_type=jnp.float32,
            )
            att[rows, key_cols[h]] = out.astype(jnp.bfloat16)
        for x, g, (_, place, _, _, h) in zip(q, grad_scores, items):
            acc[place, key_cols[h]] += dot(x, g, TN)
        return carry

    lax.fori_loop(0, (amount + TOGETHER - 1) // TOGETHER, step, 0)

    copies = [
        pltpu.make_async_copy(att.at[pl.ds(i * tokens, tokens)], out.at[i], semaphores.at[i])
        for i in range(devices)
    ]
    if not last:
        copies.append(pltpu.make_async_copy(acc, grad_outs[0], semaphores.at[devices]))
    for copy in copies:
        copy.start()
    if last:
        for i, ref in enumerate(grad_outs[: N_Z - 1]):
            ref[...] = acc[i].astype(jnp.bfloat16)
        for i, ref in enumerate(grad_outs[N_Z - 1 :]):
            ref[...] = acc[N_Z - 1, i * width // 2 : (i + 1) * width // 2].astype(jnp.bfloat16)
    for copy in copies:
        copy.wait()


def attend(work, ids, spans, tokens, parts, earlier=None):
    seen, width = parts[0].shape[0], parts[0].shape[1] // 2
    heads, last, devices = width // D_HEAD, earlier is not None, spans.shape[0]
    rows = devices * tokens
    operands = [spans, *parts] + ([earlier] if last else [])
    anywhere = pl.BlockSpec(memory_space=pl.ANY)
    sums = jax.ShapeDtypeStruct((N_Z, width, seen), jnp.float32)
    shapes = [(width, seen)] * (N_Z - 1) + [(width // 2, seen)] * 2
    out = pl.pallas_call(
        functools.partial(attention_kernel, heads, last),
        grid_spec=pltpu.PrefetchScalarGridSpec(
            num_scalar_prefetch=4,
            grid=(1,),
            in_specs=[anywhere] * len(operands),
            out_specs=[anywhere]
            + ([pl.BlockSpec(shape, lambda i, *_: (0, 0)) for shape in shapes] if last else [anywhere]),
            scratch_shapes=[
                pltpu.VMEM((2, rows, width), jnp.bfloat16),
                pltpu.VMEM((N_Z, seen, 2 * width), jnp.bfloat16),
                pltpu.VMEM((N_Z, width, seen), jnp.float32),
                pltpu.VMEM((rows, width), jnp.bfloat16),
                pltpu.SemaphoreType.DMA((2 * devices + N_Z + 2,)),
            ],
        ),
        out_shape=[jax.ShapeDtypeStruct((devices, tokens, width), jnp.bfloat16)]
        + ([jax.ShapeDtypeStruct(shape, jnp.bfloat16) for shape in shapes] if last else [sums]),
        compiler_params=pltpu.CompilerParams(vmem_limit_bytes=50 * 1024 * 1024),
        cost_estimate=pl.CostEstimate(
            flops=rows * seen * width * 2,
            bytes_accessed=rows * width * 6 + N_Z * seen * width * 10,
            transcendentals=rows * seen * heads // 4,
        ),
    )(*work, ids, *operands)
    return out[0], list(out[1:])


def normed_store(database, norm_gain):
    rows = database.reshape(-1, database.shape[2])
    stored = rows.shape[0]
    top = lax.reduce_precision(norm_gain, 8, 7)
    middle = lax.reduce_precision(norm_gain - top, 8, 7)
    bottom = norm_gain - top - middle
    gains = jnp.stack([top, middle, bottom]).astype(jnp.bfloat16)
    packed = jnp.concatenate([rows, jnp.pad(gains, ((0, 13), (0, 0)))], axis=0)
    whole = lax.all_gather(packed, "tp", axis=1, tiled=True).astype(jnp.float32)
    floats = whole[:stored]
    gain = whole[stored] + whole[stored + 1] + whole[stored + 2]
    mean = jnp.sum(floats * floats, axis=1, keepdims=True) / floats.shape[1]
    return (floats * lax.rsqrt(mean + epsilon) * gain[None, :]).astype(jnp.bfloat16)


def core_rows(x, core):
    return lax.dynamic_index_in_dim(x.reshape(x.shape[0], CHIPS, 2, -1), core, 2, False)


def scatter_gradient(total, rows):
    width = total.shape[1]
    for groups in (Y_GROUPS, Z_GROUPS):
        size = len(groups[0])
        total = total.astype(jnp.bfloat16).reshape(size, -1, rows, width)
        total = lax.all_to_all(total, "seq", 0, 0, axis_index_groups=groups, tiled=True)
        total = jnp.sum(total.astype(jnp.float32), axis=0)
    return total.reshape(rows, width)


def per_device(
    queries, cotangent, owner_map, neighbour_ids, database, norm_gain, key_weight, value_weight
):
    index = lax.axis_index("seq")
    core, here_y, here_z = index % 2, index // (2 * N_Z), index // 2 % N_Z
    tokens, local_width = queries.shape

    half = tokens // 2
    with jax.named_scope("spans"):
        meta = jnp.concatenate([owner_map, neighbour_ids], axis=1).T.astype(jnp.bfloat16)
        meta = meta.reshape(3, 2, -1)
        meta = jnp.pad(meta, ((0, 13), (0, 0), (0, local_width - meta.shape[2])))
        lines = []
        for i in range(2):
            rows = slice(i * half, (i + 1) * half)
            line = jnp.concatenate([queries[rows], cotangent[rows], meta[:, i]], axis=0)
            lines.append(lax.all_gather(line, "seq", axis_index_groups=LINES, axis=0, tiled=False))

    normed = normed_store(database, norm_gain)
    key_rows = jnp.dot(normed, key_weight, preferred_element_type=jnp.float32).astype(jnp.bfloat16)
    value_rows = jnp.dot(normed, value_weight, preferred_element_type=jnp.float32).astype(
        jnp.bfloat16
    )

    chip_normed = [core_rows(normed, core), swap(core_rows(normed, 1 - core))]
    chip_normed = jnp.concatenate(chip_normed, axis=0).reshape(2 * normed.shape[0], -1)

    with jax.named_scope("keys_values"):
        kv = jnp.concatenate([key_rows, value_rows], axis=1)
        kv = ring_near(kv, from_z, N_Z)
        kv += ring_far(kv, from_z)

    sums, attended = None, []
    for line in lines:
        if sums is not None:
            line = after(line, (sums[0], att))
        meta = line[:, tokens : tokens + 3, : half // SPAN].astype(jnp.int32)
        owners, ids = meta[:, 0].reshape(-1), meta[:, 1:].transpose(0, 2, 1).reshape(-1)
        member = (owners % 2 == core) & (owners // (2 * N_Z) == here_y)
        work = work_list(ring_place(owners // 2 - here_z, N_Z), member)
        with jax.named_scope("attend"):
            att, sums = attend(work, ids, line, half, kv, None if sums is None else sums[0])
        with jax.named_scope("attended"):
            att = att.reshape(N_Y, 2, -1, local_width)
            ours, theirs = (
                lax.dynamic_index_in_dim(att, which, 1, False) for which in (core, 1 - core)
            )
            att = ours + swap(theirs)
            attended.append(
                lax.psum_scatter(
                    att, "seq", axis_index_groups=Y_GROUPS, scatter_dimension=0, tiled=False
                )
            )
    with jax.named_scope("key_gradients"):
        grad_keys = ring_scatter(sums, from_z, N_Z)

    grad_keys = jnp.concatenate([grad_keys, swap(grad_keys)], axis=1)
    grad = lax.dot_general(
        chip_normed, grad_keys, (((0,), (1,)), ((), ())), preferred_element_type=jnp.float32
    )
    grad = scatter_gradient(grad, normed.shape[1] // (2 * CHIPS))
    return jnp.concatenate(attended, axis=0), grad


def solution(mesh):
    placed = (
        P("seq", "tp"),
        P("seq", "tp"),
        P("seq", None),
        P("seq", None),
        P("seq", None, "tp"),
        P("tp"),
        P(None, "tp"),
        P(None, "tp"),
    )
    return jax.shard_map(
        per_device,
        mesh=mesh,
        in_specs=placed,
        out_specs=(P("seq", "tp"), P("seq", "tp")),
        check_vma=False,
    )
```
